1024 devices in a mesh: dp: 16 (over z, core), ep: 8 (over y), tp: 8 (over x).
Axes of the slice: x: 8, y: 8, z: 8, core: 2. Of those that a mesh axis runs over, the one named last changes fastest.
Arguments:
- grad_out: bfloat16 [4096, 7168], P(('dp', 'ep'), 'tp'), may hold values from -6 to 6
- expert_ids: int32 [4096, 4], P(('dp', 'ep')), may hold values from 0 to 7, all different within a row; in each aligned block of 32 rows (0 to 31, 32 to 63, ...) at most 32 rows name the same one
- gate_values: bfloat16 [4096, 4], P(('dp', 'ep')), may hold values from 0.099609375 to 1
- pre_gate: bfloat16 [8, 4096, 2048], P('ep', 'dp', 'tp'), may hold values from -8 to 8
- pre_up: bfloat16 [8, 4096, 2048], P('ep', 'dp', 'tp'), may hold values from -6 to 6
- down_weight: bfloat16 [8, 2048, 7168], P('ep', 'tp'), may hold values from -0.125 to 0.125
Outputs:
- grad_pre_gate: bfloat16 [8, 4096, 2048], P('ep', 'dp', 'tp')
- grad_pre_up: bfloat16 [8, 4096, 2048], P('ep', 'dp', 'tp')
- grad_down: float32 [8, 2048, 7168], P('ep', 'tp', 'dp')
- grad_gates: float32 [8, 4096], P('ep', 'dp')
The draws below stay inside these ranges and needn't reach their ends.
Inputs may be any that keep to these rules, and one draw needn't show every extreme that they name: `expert_ids`: each token names 4 different experts. The 32 tokens of one block name one expert at most 32 times, a bound that some block reaches.
All inputs are finite; a program needn't handle non-finite values.
Results may differ from the reference program's by a relative error of at most 0.02.
Values may be sent and summed in bfloat16 or wider, within the bound.
A program may use at most 64 MiB of HBM per device.

```python
import math
import jax
import jax.numpy as jnp
import numpy as np
from jax import lax

D = 7168
HIDDEN_SIZE = 2048
TOPK = 4
TOK_DEV = 32
EXPERTS = 8
CAP = 32
TOKENS = 4096
GROUP_SLOTS = 4096
N_DP = 16
N_EP = 8


def levels(stream_key, shape, pieces, least, top_value):
    gain = 1.0
    for position, parts in pieces:
        draws = jax.random.uniform(jax.random.fold_in(jax.random.fold_in(stream_key, 6), position), (parts,), jnp.float32, least / len(pieces), top_value / len(pieces))
        gain = gain * jnp.repeat(jnp.exp(draws), shape[position] // parts).reshape((-1,) + (1,) * (len(shape) - 1 - position))
    return gain


def routed_block(key, own, number, rows, number_of, top, bound, slope):
    sequence = jax.random.permutation(key, number_of)
    packed, usual = portions_of(number_of, rows * top, bound, slope, True), portions_of(number_of, rows * top, bound, slope, False)
    places = jnp.arange(number_of)

    def named(sizes, offset_by):
        used = int((sizes > 0).sum())
        fixed = max(1, used // 4)
        moved = fixed + (places - fixed + offset_by * (used - fixed)) % max(1, number_of - fixed)
        return jnp.zeros((number_of,), jnp.int32).at[sequence[jnp.where(places < fixed, places, moved)]].set(jnp.asarray(sizes, jnp.int32))

    sizes = jnp.where(number % 4 == 0, named(packed, number // 4), named(usual, number - number // 4 - 1))
    mixed = jax.random.permutation(jax.random.fold_in(own, 3), number_of)
    giver, receiver = mixed[0:number_of // 2 * 2:2], mixed[1:number_of // 2 * 2:2]
    margin = jnp.minimum(sizes[giver] - 1, bound - sizes[receiver]) // 2
    margin = jnp.where((giver == sequence[0]) | (receiver == sequence[0]) | (sizes[receiver] == 0), 0, jnp.maximum(margin, 0))
    moved = jax.random.randint(jax.random.fold_in(own, 4), (number_of // 2,), 0, 1 << 20) % (margin + 1)
    sizes = sizes.at[giver].add(-moved).at[receiver].add(moved)
    items = jnp.searchsorted(jnp.cumsum(sizes), jnp.arange(rows * top), side="right").astype(jnp.int32)
    listing = items.reshape(top, rows).T
    listing = listing[jax.random.permutation(jax.random.fold_in(own, 1), rows)]
    offset_by = jax.random.randint(jax.random.fold_in(own, 2), (rows, 1), 0, top)
    return jnp.take_along_axis(listing, (jnp.arange(top)[None, :] + offset_by) % top, axis=1)


def portions_of(amount, total, reach, lean, full):
    loads = [(1 << 20) // math.isqrt(standing ** lean) + 1 for standing in range(1, amount + 1)]
    largest = reach if full else min(reach, max(-(-total // amount), total * loads[0] // sum(loads)))
    least = 1 if total - largest >= amount - 1 else 0
    given, spare = [largest] + [least] * (amount - 1), total - largest - least * (amount - 1)
    while spare > 0:
        candidates = [i for i in range(1, amount) if given[i] < largest] or [i for i in range(1, amount) if given[i] < reach]
        mass, remaining = sum([loads[i] for i in candidates]), spare
        for i in candidates:
            more = min(reach - given[i], max(1, remaining * loads[i] // mass), spare)
            given[i] = given[i] + more
            spare = spare - more
    return np.array(given)


def noise(rng, dims, scale, reach, cuts=(), kind=jnp.bfloat16):
    factor_of = levels(rng, dims, cuts, -0.22, 0.18) if cuts else 1.0
    drawn = jax.random.normal(rng, dims, jnp.float32) * scale * factor_of
    return jnp.minimum(jnp.maximum(drawn, -reach), reach).astype(kind)


def setup_inputs(seed: int = 0) -> dict:
    keys = jax.random.split(jax.random.key(seed), 7)
    grad_out = noise(keys[0], (TOKENS, D), 1.0, 6.0, ((0, 128), (1, 8)))
    expert_ids_keys = jax.random.split(jax.random.fold_in(keys[1], 1), TOKENS // TOK_DEV)
    expert_ids_turns = jax.random.permutation(jax.random.fold_in(keys[1], 3), TOKENS // TOK_DEV)
    expert_ids = jax.vmap(lambda own, number: routed_block(jax.random.fold_in(keys[1], 2), own, number, TOK_DEV, EXPERTS, TOPK, CAP, 2))(expert_ids_keys, expert_ids_turns).reshape((TOKENS, TOPK))
    gate_values = jnp.clip(0.099609375 + 0.9003906 * jax.random.uniform(keys[2], (TOKENS, TOPK), jnp.float32) ** levels(keys[2], (TOKENS, TOPK), ((0, 128),), -0.2, 0.2), 0.099609375, 1.0).astype(jnp.bfloat16)
    pre_gate = noise(keys[3], (EXPERTS, GROUP_SLOTS, HIDDEN_SIZE), 1.5, 8.0, ((0, 8), (1, 16), (2, 8)))
    pre_up = noise(keys[4], (EXPERTS, GROUP_SLOTS, HIDDEN_SIZE), 1.0, 6.0, ((0, 8), (1, 16), (2, 8)))
    down_weight = noise(keys[5], (EXPERTS, HIDDEN_SIZE, D), HIDDEN_SIZE ** -0.5, 0.125, ((0, 8), (1, 8)))
    return dict(grad_out=grad_out, expert_ids=expert_ids, gate_values=gate_values, pre_gate=pre_gate, pre_up=pre_up, down_weight=down_weight)


def reference(grad_out, expert_ids, gate_values, pre_gate, pre_up, down_weight):
    blocks = N_DP * N_EP
    labels = jnp.arange(EXPERTS, dtype=jnp.int32)
    onehot = (expert_ids[:, :, None] == labels[None, None, :]).astype(jnp.int32)
    hits = jnp.sum(onehot, axis=1).reshape(blocks, TOK_DEV, EXPERTS)
    ranks = (jnp.cumsum(hits, axis=1) - hits).reshape(blocks * TOK_DEV, EXPERTS)
    slot_rank = jnp.sum(onehot * ranks[:, None, :], axis=2).astype(jnp.int32)
    owner = jnp.arange(TOKENS, dtype=jnp.int32) // TOK_DEV
    slot_row = (owner[:, None] * CAP + slot_rank).astype(jnp.int32)
    flat_expert = expert_ids.reshape(-1).astype(jnp.int32)
    flat_row = slot_row.reshape(-1)
    token_of = jnp.repeat(jnp.arange(TOKENS, dtype=jnp.int32), TOPK)
    routed = jnp.zeros((EXPERTS, GROUP_SLOTS, D), jnp.bfloat16).at[flat_expert, flat_row].set(grad_out[token_of])
    scale = jnp.zeros((EXPERTS, GROUP_SLOTS), jnp.float32).at[flat_expert, flat_row].set(gate_values.reshape(-1).astype(jnp.float32))

    def one_expert(item):
        rows, gates, gate_pre, up_pre, weight = item
        first = gate_pre.astype(jnp.float32)
        second = up_pre.astype(jnp.float32)
        sigma = jax.nn.sigmoid(first)
        silu_val = first * sigma
        act = (silu_val * second).astype(jnp.bfloat16)
        back = jnp.dot(rows, weight.T, preferred_element_type=jnp.float32)
        gate_grad = jnp.sum(back * act.astype(jnp.float32), axis=1)
        grad_act = gates[:, None] * back
        grad_gate_pre = (grad_act * second * sigma * (1.0 + first * (1.0 - sigma))).astype(jnp.bfloat16)
        grad_up_pre = (grad_act * silu_val).astype(jnp.bfloat16)
        scaled = (gates[:, None] * rows.astype(jnp.float32)).astype(jnp.bfloat16)
        act_groups = act.reshape(N_DP, N_EP * CAP, HIDDEN_SIZE)
        scaled_groups = scaled.reshape(N_DP, N_EP * CAP, D)

        def add_group(total, pair):
            part = jnp.dot(pair[0].T, pair[1], preferred_element_type=jnp.float32).astype(jnp.bfloat16)
            part = lax.optimization_barrier(part)
            return total + part.astype(jnp.float32), None

        down, _ = lax.scan(add_group, jnp.zeros((HIDDEN_SIZE, D), jnp.float32), (act_groups, scaled_groups))
        return grad_gate_pre, grad_up_pre, down, gate_grad

    grad_pre_gate, grad_pre_up, grad_down, grad_gates = lax.map(one_expert, (routed, scale, pre_gate, pre_up, down_weight))
    return grad_pre_gate, grad_pre_up, grad_down, grad_gates
```

```python
import functools

import jax
import jax.numpy as jnp
from jax import lax
from jax.experimental import pallas as pl
from jax.experimental.pallas import tpu as pltpu
from jax.sharding import PartitionSpec as P

MESH = pl.DeviceIdType.MESH
F32 = jnp.float32
BF16 = jnp.bfloat16
LANE = 128
STAGES = 4
ROWS = ((0, 32), (32, 32), (64, 32), (96, 16))
SLAB = 112


def dot(a, b, dims=((1,), (0,))):
    return lax.dot_general(a, b, (dims, ((), ())), preferred_element_type=F32)


def kernel(
    nx, ny, nz,
    grad_ref, ids_ref, gate_ref, pg_hbm, pu_hbm, w_hbm,
    dpg_ref, dpu_ref, down_ref, dgate_ref,
    ta, tb, meta, w, pg, pu, act, st, sm, at, am, gslot, back,
    own, away, mate, own3, away3, mate3,
    out_r, in_r, out_3, in_3, dots,
    sem_local, p1_send, p1_recv, meta_send, meta_recv,
    ag_send, ag_recv, mate_send, mate_recv, rs_send, rs_recv, dot_send, dot_recv,
):
    tok = grad_ref.shape[0]
    rows = ny * tok
    hidden = pg.shape[1]
    x, y, dp = lax.axis_index("tp"), lax.axis_index("ep"), lax.axis_index("dp")
    z, core = dp // 2, dp % 2
    kx, ky, kz = nx // 2, ny // 2, nz // 2
    assert kx == nx // 2 and nx == nz

    def at_x(d):
        return {"tp": lax.rem(x + d + nx, nx)}

    def at_y(d):
        return {"ep": lax.rem(y + d + ny, ny)}

    def at_z(d):
        return {"dp": lax.rem(z + d + nz, nz) * 2 + core}

    other = {"dp": z * 2 + 1 - core}

    barrier = pltpu.get_barrier_semaphore()
    peers = [at_x(k) for k in range(1, nx)] + [at_y(k) for k in range(1, ny)] + [other]
    peers += [at_z(1), at_z(-1)]
    for peer in peers:
        pl.semaphore_signal(barrier, inc=1, device_id=peer, device_id_type=MESH)

    locals_ = [
        pltpu.make_async_copy(pg_hbm.at[0], pg, sem_local.at[0]),
        pltpu.make_async_copy(pu_hbm.at[0], pu, sem_local.at[1]),
        pltpu.make_async_copy(w_hbm.at[0], w, sem_local.at[2]),
    ]
    for c in locals_:
        c.start()

    for s in range(3):
        ta[x, y, 32 * s:32 * s + 32, :] = grad_ref[:, LANE * s:LANE * (s + 1)]
        tb[x, y, 32 * s:32 * s + 32, :] = grad_ref[:, LANE * (s + 4):LANE * (s + 5)]
    ta[x, y, 96:112, :] = grad_ref[0:16, 3 * LANE:4 * LANE]
    tb[x, y, 96:112, :] = grad_ref[16:32, 3 * LANE:4 * LANE]
    lanes = lax.broadcasted_iota(jnp.int32, (tok, LANE), 1)
    table = jnp.zeros((tok, LANE), F32)
    gates = gate_ref[...].astype(F32)
    for k in range(ids_ref.shape[1]):
        named = ids_ref[:, k:k + 1]
        table = jnp.where(lanes == named, gates[:, k:k + 1], table)
        table = jnp.where(lanes == named + 64, 1.0, table)
    meta[y] = table.astype(BF16)

    pl.semaphore_wait(barrier, len(peers))

    def p1(path, part, k):
        lo, n = (0, 32) if part == 0 else (32, SLAB - 32)
        buf = ta if path == 0 else tb
        ref = buf.at[x, y, pl.ds(lo, n), :]
        return pltpu.make_async_remote_copy(
            src_ref=ref, dst_ref=ref,
            send_sem=p1_send.at[path, part, k], recv_sem=p1_recv.at[path, part, k],
            device_id=at_y(k) if path == 0 else at_x(k), device_id_type=MESH,
        )

    def meta_copy(k):
        return pltpu.make_async_remote_copy(
            src_ref=meta.at[y], dst_ref=meta.at[y],
            send_sem=meta_send.at[k], recv_sem=meta_recv.at[k],
            device_id=at_y(k), device_id_type=MESH,
        )

    p1_all = [(0, k) for k in range(1, ny)] + [(1, k) for k in range(1, nx)]
    for path, k in p1_all:
        p1(path, 0, k).start()
    for k in range(1, ny):
        meta_copy(k).start()
    for path, k in p1_all:
        p1(path, 1, k).start()

    def ag(s, k, path, right):
        lo, n = ROWS[s]
        last = k == (kx if path == 0 else ky) - 1
        step = -k if right else k
        if path == 0:
            half = ny // 2
            span = pl.ds(0 if right else half, half) if last else pl.ds(0, ny)
            ref = ta.at[lax.rem(x + step + nx, nx), span, pl.ds(lo, n), :]
            to = at_x(1 if right else -1)
        else:
            half = nx // 2
            span = pl.ds(0 if right else half, half) if last else pl.ds(0, nx)
            ref = tb.at[span, lax.rem(y + step + ny, ny), pl.ds(lo, n), :]
            to = at_y(1 if right else -1)
        return pltpu.make_async_remote_copy(
            src_ref=ref, dst_ref=ref,
            send_sem=ag_send.at[s, k, path, int(right)],
            recv_sem=ag_recv.at[s, k, path, int(right)],
            device_id=to, device_id_type=MESH,
        )

    steps = max(kx, ky)

    def streams(k):
        return [(p, r) for p in (0, 1) for r in (True, False) if k < (kx if p == 0 else ky)]

    def ag_start(s, k):
        for p, r in streams(k):
            if k > 0:
                ag(s, k - 1, p, r).wait_recv()
            ag(s, k, p, r).start()

    def ag_finish(s):
        for p in (0, 1):
            for r in (True, False):
                ag(s, (kx if p == 0 else ky) - 1, p, r).wait_recv()

    def prepare():
        locals_[0].wait()
        locals_[1].wait()
        gate_pre = pg[...].astype(F32)
        up_pre = pu[...].astype(F32)
        sigma = jax.nn.sigmoid(gate_pre)
        act[...] = (gate_pre * sigma * up_pre).astype(BF16)
        for k in range(1, ny):
            meta_copy(k).wait_recv()
        tables = meta[...].reshape(rows, LANE)
        tables32 = tables.astype(F32)
        at_row = lax.broadcasted_iota(jnp.int32, (rows, rows), 0)
        at_col = lax.broadcasted_iota(jnp.int32, (rows, rows), 1)
        before = (at_row // tok == at_col // tok) & (at_col < at_row)
        before = jnp.where(before, 1.0, 0.0).astype(BF16)
        ranks = dot(before, tables)
        lane = lax.broadcasted_iota(jnp.int32, (rows, LANE), 1)
        gate_t = jnp.sum(jnp.where(lane == y, tables32, 0.0), axis=1, keepdims=True)
        member = jnp.sum(jnp.where(lane == y + 64, tables32, 0.0), axis=1, keepdims=True)
        rank = jnp.sum(jnp.where(lane == y + 64, ranks, 0.0), axis=1, keepdims=True)
        slot = rank.astype(jnp.int32) + at_row[:, 0:1] // tok * tok
        place = jnp.where(at_col == slot, member, 0.0)
        sm32 = place.T
        sm[...] = sm32.astype(BF16)
        gslot[...] = jnp.sum(
            jnp.where(lane == y, dot(sm[...], tables), 0.0), axis=1, keepdims=True
        )
        moved = dot(place.astype(BF16), act[...]) * gate_t
        am[...] = moved.astype(BF16)
        at[...] = moved.T.astype(BF16)
        back[...] = jnp.zeros_like(back)

    def compute(s):
        if s < 3:
            def body(i, carry):
                lo = ROWS[s][0]
                left = ta[i, :, lo:lo + 32, :].reshape(rows, LANE)
                right = tb[i, :, lo:lo + 32, :].reshape(rows, LANE)
                both = jnp.concatenate([left, right], axis=1)
                first = pl.multiple_of(i * 7 * LANE + s * LANE, LANE)
                second = pl.multiple_of(i * 7 * LANE + (s + 4) * LANE, LANE)
                wide = jnp.concatenate(
                    [w[:, pl.ds(first, LANE)], w[:, pl.ds(second, LANE)]], axis=1
                )
                term = dot(at[...], both)
                mine = jnp.where(core == 0, term[:, :LANE], term[:, LANE:])
                theirs = jnp.where(core == 0, term[:, LANE:], term[:, :LANE])
                own[s, i] = mine
                away[s, i] = theirs.astype(BF16)
                back[...] += dot(both, wide, ((1,), (1,)))
                return carry
        else:
            def body(i, carry):
                lo = ROWS[s][0]
                top = ta[i, :, lo:lo + 16, :]
                low = tb[i, :, lo:lo + 16, :]
                tile = jnp.concatenate([top, low], axis=1).reshape(rows, LANE)
                first = pl.multiple_of(i * 7 * LANE + 3 * LANE, LANE)
                term = dot(tile, am[...], ((0,), (0,)))
                half = LANE // 2
                mine = jnp.where(core == 0, term[:half], term[half:])
                theirs = jnp.where(core == 0, term[half:], term[:half])
                own3[i] = mine
                away3[i] = theirs.astype(BF16)
                back[...] += dot(tile, w[:, pl.ds(first, LANE)], ((1,), (1,)))
                return carry
        lax.fori_loop(0, nx, body, 0)

    def swap(s):
        return pltpu.make_async_remote_copy(
            src_ref=away.at[s] if s < 3 else away3,
            dst_ref=mate.at[s] if s < 3 else mate3,
            send_sem=mate_send.at[s], recv_sem=mate_recv.at[s],
            device_id=other, device_id_type=MESH,
        )

    def rs(s, r, right):
        size = hidden if s < 3 else LANE // 2
        half = size // 2
        if r == 0:
            span = pl.ds(0 if right else half, half)
        else:
            span = pl.ds(0, size)
        d = int(right)
        if s < 3:
            src, dst = out_r.at[s, r, d, span, :], in_r.at[s, r, d, span, :]
        else:
            src, dst = out_3.at[r, d, span, :], in_3.at[r, d, span, :]
        return pltpu.make_async_remote_copy(
            src_ref=src, dst_ref=dst,
            send_sem=rs_send.at[s, r, d], recv_sem=rs_recv.at[s, r, d],
            device_id=at_z(1 if right else -1), device_id_type=MESH,
        )

    def chip_sum(s, o, lo, n):
        if s < 3:
            return own[s, o, lo:lo + n, :] + mate[s, o, lo:lo + n, :].astype(F32)
        return own3[o, lo:lo + n, :] + mate3[o, lo:lo + n, :].astype(F32)

    def came(s, r, d, lo, n):
        if s < 3:
            return in_r[s, r, d, lo:lo + n, :].astype(F32)
        return in_3[r, d, lo:lo + n, :].astype(F32)

    def rs_start(s, r):
        size = hidden if s < 3 else LANE // 2
        half = size // 2
        if r == 0:
            swap(s).wait_recv()
        for right in (True, False):
            d = int(right)
            o = lax.rem(z + (kz - r if right else r - kz) + nz, nz)
            if r > 0:
                rs(s, r - 1, right).wait_recv()
            for lo in (0, half):
                in_half = (lo == 0) == right
                if r == 0 and not in_half:
                    continue
                value = chip_sum(s, o, lo, half)
                if r > 1 or (r == 1 and in_half):
                    value = value + came(s, r - 1, d, lo, half)
                if s < 3:
                    out_r[s, r, d, lo:lo + half, :] = value.astype(BF16)
                else:
                    out_3[r, d, lo:lo + half, :] = value.astype(BF16)
            rs(s, r, right).start()

    def rs_finish(s):
        size = hidden if s < 3 else LANE // 2
        half = size // 2
        for right in (True, False):
            rs(s, kz - 1, right).wait_recv()
        parts = []
        for lo in (0, half):
            value = chip_sum(s, z, lo, half)
            for d in (1, 0):
                if kz > 1 or (lo == 0) == (d == 1):
                    value = value + came(s, kz - 1, d, lo, half)
            parts.append(value)
        value = jnp.concatenate(parts, axis=0)
        if s < 3:
            @pl.when(core == 0)
            def _():
                down_ref[0, :, LANE * s:LANE * (s + 1)] = value

            @pl.when(core == 1)
            def _():
                down_ref[0, :, LANE // 2 + LANE * s:LANE // 2 + LANE * (s + 1)] = value
        else:
            turned = value.T

            @pl.when(core == 0)
            def _():
                down_ref[0, :, 3 * LANE:3 * LANE + LANE // 2] = turned

            @pl.when(core == 1)
            def _():
                down_ref[0, :, 0:LANE // 2] = turned

    def dot_copy(k):
        return pltpu.make_async_remote_copy(
            src_ref=dots.at[x], dst_ref=dots.at[x],
            send_sem=dot_send.at[k], recv_sem=dot_recv.at[k],
            device_id=at_x(k), device_id_type=MESH,
        )

    def finish_slots():
        whole = back[...]
        high = whole.astype(BF16)
        low = (whole - high.astype(F32)).astype(BF16)
        placed = dot(sm[...], high) + dot(sm[...], low)
        prod = placed * act[...].astype(F32)
        total = jnp.sum(prod.T, axis=0, keepdims=True)
        dots[x] = jnp.broadcast_to(total, (8, rows))
        for k in range(1, nx):
            dot_copy(k).start()
        gate_pre = pg[...].astype(F32)
        up_pre = pu[...].astype(F32)
        sigma = jax.nn.sigmoid(gate_pre)
        grad_act = gslot[...] * placed
        dpg_ref[0] = (grad_act * up_pre * sigma * (1.0 + gate_pre * (1.0 - sigma))).astype(BF16)
        dpu_ref[0] = (grad_act * (gate_pre * sigma)).astype(BF16)

    def finish_dots():
        for k in range(1, nx):
            dot_copy(k).wait_recv()
        total = dots[0]
        for i in range(1, nx):
            total = total + dots[i]
        dgate_ref[...] = total[0:1, :]

    def p1_wait(part):
        for path, k in p1_all:
            p1(path, part, k).wait_recv()

    for t in range(2 * STAGES + steps + kz + 2):
        for s in range(STAGES):
            k = t - 2 * s
            if 0 <= k < steps:
                if s <= 1 and k == 0:
                    p1_wait(s)
                ag_start(s, k)
            if k == steps:
                ag_finish(s)
            r = k - steps - 1
            if 0 <= r < kz:
                rs_start(s, r)
            if r == kz:
                rs_finish(s)
        if t == 0:
            prepare()
            locals_[2].wait()
        for s in range(STAGES):
            if t - 2 * s == steps:
                compute(s)
                swap(s).start()
                if s == STAGES - 1:
                    finish_slots()
    finish_dots()

    for path, k in p1_all:
        for part in (0, 1):
            p1(path, part, k).wait_send()
    for k in range(1, ny):
        meta_copy(k).wait_send()
    for s in range(STAGES):
        for k in range(steps):
            for p, r in streams(k):
                ag(s, k, p, r).wait_send()
        swap(s).wait_send()
        for r in range(kz):
            for right in (True, False):
                rs(s, r, right).wait_send()
    for k in range(1, nx):
        dot_copy(k).wait_send()


def solution(mesh):
    nx, ny, nz = mesh.shape["tp"], mesh.shape["ep"], mesh.shape["dp"] // 2
    steps = max(nx, ny) // 2

    def local(grad_out, expert_ids, gate_values, pre_gate, pre_up, down_weight):
        rows, hidden = pre_gate.shape[1:]
        width = down_weight.shape[2]
        tok = grad_out.shape[0]
        half = LANE // 2
        kz = nz // 2
        dma = pltpu.SemaphoreType.DMA
        vmem = pl.BlockSpec(memory_space=pltpu.VMEM)
        hbm = pl.BlockSpec(memory_space=pl.ANY)
        return pl.pallas_call(
            functools.partial(kernel, nx, ny, nz),
            out_shape=(
                jax.ShapeDtypeStruct(pre_gate.shape, BF16),
                jax.ShapeDtypeStruct(pre_up.shape, BF16),
                jax.ShapeDtypeStruct((1, hidden, width // (2 * nz)), F32),
                jax.ShapeDtypeStruct((1, rows), F32),
            ),
            in_specs=[vmem, vmem, vmem, hbm, hbm, hbm],
            out_specs=(vmem, vmem, vmem, vmem),
            scratch_shapes=[
                pltpu.VMEM((nx, ny, SLAB, LANE), BF16),
                pltpu.VMEM((nx, ny, SLAB, LANE), BF16),
                pltpu.VMEM((ny, tok, LANE), BF16),
                pltpu.VMEM((hidden, width), BF16),
                pltpu.VMEM((rows, hidden), BF16),
                pltpu.VMEM((rows, hidden), BF16),
                pltpu.VMEM((rows, hidden), BF16),
                pltpu.VMEM((rows, rows), BF16),
                pltpu.VMEM((rows, rows), BF16),
                pltpu.VMEM((hidden, rows), BF16),
                pltpu.VMEM((rows, hidden), BF16),
                pltpu.VMEM((rows, 1), F32),
                pltpu.VMEM((rows, hidden), F32),
                pltpu.VMEM((3, nx, hidden, LANE), F32),
                pltpu.VMEM((3, nx, hidden, LANE), BF16),
                pltpu.VMEM((3, nx, hidden, LANE), BF16),
                pltpu.VMEM((nx, half, hidden), F32),
                pltpu.VMEM((nx, half, hidden), BF16),
                pltpu.VMEM((nx, half, hidden), BF16),
                pltpu.VMEM((3, kz, 2, hidden, LANE), BF16),
                pltpu.VMEM((3, kz, 2, hidden, LANE), BF16),
                pltpu.VMEM((kz, 2, half, hidden), BF16),
                pltpu.VMEM((kz, 2, half, hidden), BF16),
                pltpu.VMEM((nx, 8, rows), F32),
                dma((3,)),
                dma((2, 2, max(nx, ny))),
                dma((2, 2, max(nx, ny))),
                dma((ny,)),
                dma((ny,)),
                dma((STAGES, steps, 2, 2)),
                dma((STAGES, steps, 2, 2)),
                dma((STAGES,)),
                dma((STAGES,)),
                dma((STAGES, kz, 2)),
                dma((STAGES, kz, 2)),
                dma((nx,)),
                dma((nx,)),
            ],
            compiler_params=pltpu.CompilerParams(
                collective_id=0, has_side_effects=True, vmem_limit_bytes=48 * 1024 * 1024
            ),
        )(grad_out, expert_ids, gate_values, pre_gate, pre_up, down_weight)

    placed = (
        P(("dp", "ep"), "tp"),
        P(("dp", "ep"), None),
        P(("dp", "ep"), None),
        P("ep", "dp", "tp"),
        P("ep", "dp", "tp"),
        P("ep", "tp", None),
    )
    return jax.shard_map(
        local,
        mesh=mesh,
        in_specs=placed,
        out_specs=(P("ep", "dp", "tp"), P("ep", "dp", "tp"), P("ep", "tp", "dp"), P("ep", "dp")),
        check_vma=False,
    )
```

```python
import functools

import jax
import jax.numpy as jnp
from jax import lax
from jax.experimental import pallas as pl
from jax.experimental.pallas import tpu as pltpu
from jax.sharding import PartitionSpec as P

MESH = pl.DeviceIdType.MESH
F32 = jnp.float32
BF16 = jnp.bfloat16
LANE = 128
STAGES = 4
ROWS = ((0, 32), (32, 32), (64, 32), (96, 16))
SLAB = 112


def dot(a, b, dims=((1,), (0,))):
    return lax.dot_general(a, b, (dims, ((), ())), preferred_element_type=F32)


def kernel(
    nx, ny, nz,
    grad_hbm, ids_hbm, gate_hbm, pg_hbm, pu_hbm, w_hbm,
    dpg_hbm, dpu_hbm, down_hbm, dgate_ref,
    grad_ref, ids_ref, gate_ref,
    ta, tb, meta, w, pg, pu, act, sm, at, am, gslot, back,
    own, away, mate, own3, away3, mate3,
    out_r, in_r, out_3, in_3, dots, dpg_ref, dpu_ref, down_ref,
    sem_local, sem_out, p1_send, p1_recv, meta_send, meta_recv,
    ag_send, ag_recv, mate_send, mate_recv, rs_send, rs_recv, dot_send, dot_recv,
):
    tok = grad_ref.shape[0]
    rows = ny * tok
    hidden = pg.shape[1]
    x, y, dp = lax.axis_index("tp"), lax.axis_index("ep"), lax.axis_index("dp")
    z, core = dp // 2, dp % 2
    kx, ky, kz = nx // 2, ny // 2, nz // 2
    assert kx == nx // 2 and nx == nz

    def at_x(d):
        return {"tp": lax.rem(x + d + nx, nx)}

    def at_y(d):
        return {"ep": lax.rem(y + d + ny, ny)}

    def at_z(d):
        return {"dp": lax.rem(z + d + nz, nz) * 2 + core}

    other = {"dp": z * 2 + 1 - core}

    barrier = pltpu.get_barrier_semaphore()
    peers = [at_x(k) for k in range(1, nx)] + [at_y(k) for k in range(1, ny)] + [other]
    peers += [at_z(1), at_z(-1)]
    for peer in peers:
        pl.semaphore_signal(barrier, inc=1, device_id=peer, device_id_type=MESH)

    first = [
        pltpu.make_async_copy(grad_hbm, grad_ref, sem_local.at[3]),
        pltpu.make_async_copy(ids_hbm, ids_ref, sem_local.at[4]),
        pltpu.make_async_copy(gate_hbm, gate_ref, sem_local.at[5]),
    ]
    for c in first:
        c.start()
    locals_ = [
        pltpu.make_async_copy(pg_hbm.at[0], pg, sem_local.at[0]),
        pltpu.make_async_copy(pu_hbm.at[0], pu, sem_local.at[1]),
        pltpu.make_async_copy(w_hbm.at[0], w, sem_local.at[2]),
    ]
    for c in locals_:
        c.start()

    for c in first:
        c.wait()
    for s in range(3):
        ta[x, y, 32 * s:32 * s + 32, :] = grad_ref[:, LANE * s:LANE * (s + 1)]
        tb[x, y, 32 * s:32 * s + 32, :] = grad_ref[:, LANE * (s + 4):LANE * (s + 5)]
    ta[x, y, 96:112, :] = grad_ref[0:16, 3 * LANE:4 * LANE]
    tb[x, y, 96:112, :] = grad_ref[16:32, 3 * LANE:4 * LANE]
    labels = lax.broadcasted_iota(jnp.int32, (LANE, tok), 0)
    table = jnp.zeros((LANE, tok), F32)
    gates = gate_ref[...].astype(F32)
    for k in range(ids_ref.shape[0]):
        named = ids_ref[k:k + 1, :]
        table = jnp.where(labels == named, gates[k:k + 1, :], table)
        table = jnp.where(labels == named + 64, 1.0, table)
    meta[y] = table.T.astype(BF16)

    pl.semaphore_wait(barrier, len(peers))

    def p1(path, part, k):
        lo, n = (0, 32) if part == 0 else (32, SLAB - 32)
        buf = ta if path == 0 else tb
        ref = buf.at[x, y, pl.ds(lo, n), :]
        return pltpu.make_async_remote_copy(
            src_ref=ref, dst_ref=ref,
            send_sem=p1_send.at[path, part, k], recv_sem=p1_recv.at[path, part, k],
            device_id=at_y(k) if path == 0 else at_x(k), device_id_type=MESH,
        )

    def meta_copy(k):
        return pltpu.make_async_remote_copy(
            src_ref=meta.at[y], dst_ref=meta.at[y],
            send_sem=meta_send.at[k], recv_sem=meta_recv.at[k],
            device_id=at_y(k), device_id_type=MESH,
        )

    p1_all = [(0, k) for k in range(1, ny)] + [(1, k) for k in range(1, nx)]
    p1_all.sort(key=lambda e: abs(e[1] - (ny if e[0] == 0 else nx) // 2))
    for path, k in p1_all:
        p1(path, 0, k).start()
    for k in range(1, ny):
        meta_copy(k).start()
    for path, k in p1_all:
        p1(path, 1, k).start()

    def ag(s, k, path, right):
        lo, n = ROWS[s]
        last = k == (kx if path == 0 else ky) - 1
        step = -k if right else k
        if path == 0:
            half = ny // 2
            span = pl.ds(0 if right else half, half) if last else pl.ds(0, ny)
            ref = ta.at[lax.rem(x + step + nx, nx), span, pl.ds(lo, n), :]
            to = at_x(1 if right else -1)
        else:
            half = nx // 2
            span = pl.ds(0 if right else half, half) if last else pl.ds(0, nx)
            ref = tb.at[span, lax.rem(y + step + ny, ny), pl.ds(lo, n), :]
            to = at_y(1 if right else -1)
        return pltpu.make_async_remote_copy(
            src_ref=ref, dst_ref=ref,
            send_sem=ag_send.at[s, k, path, int(right)],
            recv_sem=ag_recv.at[s, k, path, int(right)],
            device_id=to, device_id_type=MESH,
        )

    steps = max(kx, ky)

    def streams(k):
        return [(p, r) for p in (0, 1) for r in (True, False) if k < (kx if p == 0 else ky)]

    def ag_start(s, k):
        for p, r in streams(k):
            if k > 0:
                ag(s, k - 1, p, r).wait_recv()
            ag(s, k, p, r).start()

    def ag_finish(s):
        for p in (0, 1):
            for r in (True, False):
                ag(s, (kx if p == 0 else ky) - 1, p, r).wait_recv()

    def prepare():
        locals_[0].wait()
        locals_[1].wait()
        gate_pre = pg[...].astype(F32)
        up_pre = pu[...].astype(F32)
        sigma = jax.nn.sigmoid(gate_pre)
        act[...] = (gate_pre * sigma * up_pre).astype(BF16)
        for k in range(1, ny):
            meta_copy(k).wait_recv()
        tables = meta[...].reshape(rows, LANE)
        tables32 = tables.astype(F32)
        at_row = lax.broadcasted_iota(jnp.int32, (rows, rows), 0)
        at_col = lax.broadcasted_iota(jnp.int32, (rows, rows), 1)
        before = (at_row // tok == at_col // tok) & (at_col < at_row)
        before = jnp.where(before, 1.0, 0.0).astype(BF16)
        ranks = dot(before, tables)
        lane = lax.broadcasted_iota(jnp.int32, (rows, LANE), 1)
        gate_t = jnp.sum(jnp.where(lane == y, tables32, 0.0), axis=1, keepdims=True)
        member = jnp.sum(jnp.where(lane == y + 64, tables32, 0.0), axis=1, keepdims=True)
        rank = jnp.sum(jnp.where(lane == y + 64, ranks, 0.0), axis=1, keepdims=True)
        slot = rank.astype(jnp.int32) + at_row[:, 0:1] // tok * tok
        place = jnp.where(at_col == slot, member, 0.0)
        sm32 = place.T
        sm[...] = sm32.astype(BF16)
        gslot[...] = jnp.sum(
            jnp.where(lane == y, dot(sm[...], tables), 0.0), axis=1, keepdims=True
        )
        moved = dot(place.astype(BF16), act[...]) * gate_t
        am[...] = moved.astype(BF16)
        at[...] = moved.T.astype(BF16)
        back[...] = jnp.zeros_like(back)

    def owner(i):
        return lax.rem(z + lax.select(i % 2 == 1, kz - (i + 1) // 2, i // 2 - kz) + nz, nz)

    def columns(s, i):
        lo, n = ROWS[s]
        a_part, b_part = ta[i, :, lo:lo + n, :], tb[i, :, lo:lo + n, :]
        if s < 3:
            return jnp.concatenate(
                [a_part.reshape(rows, LANE), b_part.reshape(rows, LANE)], axis=1
            )
        return jnp.concatenate([a_part, b_part], axis=1).reshape(rows, LANE)

    def terms(s, lo, hi):
        half = LANE // 2

        def body(i, carry):
            block = columns(s, owner(i))
            if s < 3:
                term = dot(at[...], block)
                first, second = term[:, :LANE], term[:, LANE:]
            else:
                term = dot(block, am[...], ((0,), (0,)))
                first, second = term[:half], term[half:]
            mine = jnp.where(core == 0, first, second)
            theirs = jnp.where(core == 0, second, first).astype(BF16)
            if s < 3:
                own[s, i] = mine
                away[s, i] = theirs
            else:
                own3[i] = mine
                away3[i] = theirs
            return carry
        lax.fori_loop(lo, hi, body, 0)

    def backs(s):
        def body(i, carry):
            block = columns(s, i)
            base = i * 7 * LANE
            first = pl.multiple_of(base + s * LANE, LANE)
            weights = w[:, pl.ds(first, LANE)]
            if s < 3:
                second = pl.multiple_of(base + (s + 4) * LANE, LANE)
                weights = jnp.concatenate([weights, w[:, pl.ds(second, LANE)]], axis=1)
            back[...] += dot(block, weights, ((1,), (1,)))
            return carry
        lax.fori_loop(0, nx, body, 0)

    cut = min(3, nx - 1)

    def swap(s, part):
        span = pl.ds(0, cut) if part == 0 else pl.ds(cut, nx - cut)
        src, dst = (away.at[s], mate.at[s]) if s < 3 else (away3, mate3)
        return pltpu.make_async_remote_copy(
            src_ref=src.at[span], dst_ref=dst.at[span],
            send_sem=mate_send.at[s, part], recv_sem=mate_recv.at[s, part],
            device_id=other, device_id_type=MESH,
        )

    def rs(s, r, right):
        size = hidden if s < 3 else LANE // 2
        half = size // 2
        if r == 0:
            span = pl.ds(0 if right else half, half)
        else:
            span = pl.ds(0, size)
        d = int(right)
        if s < 3:
            src, dst = out_r.at[s, r, d, span, :], in_r.at[s, r, d, span, :]
        else:
            src, dst = out_3.at[r, d, span, :], in_3.at[r, d, span, :]
        return pltpu.make_async_remote_copy(
            src_ref=src, dst_ref=dst,
            send_sem=rs_send.at[s, r, d], recv_sem=rs_recv.at[s, r, d],
            device_id=at_z(1 if right else -1), device_id_type=MESH,
        )

    def chip_sum(s, i, lo, n):
        if s < 3:
            return own[s, i, lo:lo + n, :] + mate[s, i, lo:lo + n, :].astype(F32)
        return own3[i, lo:lo + n, :] + mate3[i, lo:lo + n, :].astype(F32)

    def came(s, r, d, lo, n):
        if s < 3:
            return in_r[s, r, d, lo:lo + n, :].astype(F32)
        return in_3[r, d, lo:lo + n, :].astype(F32)

    def rs_start(s, r):
        size = hidden if s < 3 else LANE // 2
        half = size // 2
        if r in (0, 2):
            swap(s, r // 2).wait_recv()
        for right in (True, False):
            d = int(right)
            chunk = max(2 * r - d, 0)
            if r > 0:
                rs(s, r - 1, right).wait_recv()
            for lo in (0, half):
                in_half = (lo == 0) == right
                if r == 0 and not in_half:
                    continue
                value = chip_sum(s, chunk, lo, half)
                if r > 1 or (r == 1 and in_half):
                    value = value + came(s, r - 1, d, lo, half)
                if s < 3:
                    out_r[s, r, d, lo:lo + half, :] = value.astype(BF16)
                else:
                    out_3[r, d, lo:lo + half, :] = value.astype(BF16)
            rs(s, r, right).start()

    def rs_finish(s):
        size = hidden if s < 3 else LANE // 2
        half = size // 2
        if kz <= 2:
            swap(s, 1).wait_recv()
        for right in (True, False):
            rs(s, kz - 1, right).wait_recv()
        parts = []
        for lo in (0, half):
            value = chip_sum(s, nz - 1, lo, half)
            for d in (1, 0):
                if kz > 1 or (lo == 0) == (d == 1):
                    value = value + came(s, kz - 1, d, lo, half)
            parts.append(value)
        value = jnp.concatenate(parts, axis=0)
        if s < 3:
            down_ref[s] = value.T
            down_copy(s).start()
        else:
            down_ref[s, 0:LANE // 2, :] = value
            down_copy(s).start()

    def down_copy(s):
        first = LANE * s + core * (LANE // 2) if s < 3 else (1 - core) * 3 * LANE
        size = LANE if s < 3 else LANE // 2
        return pltpu.make_async_copy(
            down_ref.at[s, pl.ds(0, size), :],
            down_hbm.at[0, pl.ds(pl.multiple_of(first, 8), size), :],
            sem_out.at[s],
        )

    slot_copies = [
        pltpu.make_async_copy(dpg_ref, dpg_hbm.at[0], sem_out.at[4]),
        pltpu.make_async_copy(dpu_ref, dpu_hbm.at[0], sem_out.at[5]),
    ]

    def dot_copy(k):
        return pltpu.make_async_remote_copy(
            src_ref=dots.at[x], dst_ref=dots.at[x],
            send_sem=dot_send.at[k], recv_sem=dot_recv.at[k],
            device_id=at_x(k), device_id_type=MESH,
        )

    def finish_slots():
        whole = back[...]
        high = whole.astype(BF16)
        low = (whole - high.astype(F32)).astype(BF16)
        placed = dot(sm[...], high) + dot(sm[...], low)
        prod = placed * act[...].astype(F32)
        total = jnp.sum(prod.T, axis=0, keepdims=True)
        dots[x] = jnp.broadcast_to(total, (8, rows))
        for k in range(1, nx):
            dot_copy(k).start()
        gate_pre = pg[...].astype(F32)
        up_pre = pu[...].astype(F32)
        sigma = jax.nn.sigmoid(gate_pre)
        grad_act = gslot[...] * placed
        dpg_ref[...] = (grad_act * up_pre * sigma * (1.0 + gate_pre * (1.0 - sigma))).astype(BF16)
        dpu_ref[...] = (grad_act * (gate_pre * sigma)).astype(BF16)
        for c in slot_copies:
            c.start()

    def finish_dots():
        for k in range(1, nx):
            dot_copy(k).wait_recv()
        total = dots[0]
        for i in range(1, nx):
            total = total + dots[i]
        dgate_ref[...] = total[0:1, :]

    def multiply(s):
        ag_finish(s)
        if s == 0:
            locals_[2].wait()
        terms(s, 0, cut)
        swap(s, 0).start()
        terms(s, cut, nx)
        swap(s, 1).start()

    def p1_wait(part):
        for path, k in p1_all:
            p1(path, part, k).wait_recv()

    plan = []
    for s in range(STAGES):
        plan += [(k + 0.4 * s, s, ag_start, k) for k in range(steps)]
        plan += [(steps + 0.4 * s, s, multiply, None)]
        plan += [(steps + 1 + 0.4 * s + r, s, rs_start, r) for r in range(kz)]
        plan += [(steps + 1 + 0.4 * s + kz, s, rs_finish, None)]
    for _, s, step, k in sorted(plan, key=lambda e: e[:2]):
        if step is ag_start and k == 0 and s <= 1:
            p1_wait(s)
        if k is None:
            step(s)
        else:
            step(s, k)
        if step is ag_start and k == 0 and s == 2:
            prepare()
        if step is rs_start and k == min(1, kz - 1):
            backs(s)
            if s == STAGES - 1:
                finish_slots()
    finish_dots()

    for path, k in p1_all:
        for part in (0, 1):
            p1(path, part, k).wait_send()
    for k in range(1, ny):
        meta_copy(k).wait_send()
    for s in range(STAGES):
        for k in range(steps):
            for p, r in streams(k):
                ag(s, k, p, r).wait_send()
        for part in (0, 1):
            swap(s, part).wait_send()
        for r in range(kz):
            for right in (True, False):
                rs(s, r, right).wait_send()
    for k in range(1, nx):
        dot_copy(k).wait_send()
    for c in slot_copies + [down_copy(s) for s in range(STAGES)]:
        c.wait()


def solution(mesh):
    nx, ny, nz = mesh.shape["tp"], mesh.shape["ep"], mesh.shape["dp"] // 2
    steps = max(nx, ny) // 2

    def local(grad_out, expert_ids, gate_values, pre_gate, pre_up, down_weight):
        rows, hidden = pre_gate.shape[1:]
        width = down_weight.shape[2]
        tok = grad_out.shape[0]
        half = LANE // 2
        kz = nz // 2
        dma = pltpu.SemaphoreType.DMA
        vmem = pl.BlockSpec(memory_space=pltpu.VMEM)
        hbm = pl.BlockSpec(memory_space=pltpu.HBM)
        outs = pl.pallas_call(
            functools.partial(kernel, nx, ny, nz),
            out_shape=(
                jax.ShapeDtypeStruct(pre_gate.shape, BF16),
                jax.ShapeDtypeStruct(pre_up.shape, BF16),
                jax.ShapeDtypeStruct((1, width // (2 * nz), hidden), F32),
                jax.ShapeDtypeStruct((1, rows), F32),
            ),
            in_specs=[hbm] * 6,
            out_specs=(hbm, hbm, hbm, vmem),
            scratch_shapes=[
                pltpu.VMEM(grad_out.shape, BF16),
                pltpu.VMEM(expert_ids.shape[::-1], jnp.int32),
                pltpu.VMEM(gate_values.shape[::-1], BF16),
                pltpu.VMEM((nx, ny, SLAB, LANE), BF16),
                pltpu.VMEM((nx, ny, SLAB, LANE), BF16),
                pltpu.VMEM((ny, tok, LANE), BF16),
                pltpu.VMEM((hidden, width), BF16),
                pltpu.VMEM((rows, hidden), BF16),
                pltpu.VMEM((rows, hidden), BF16),
                pltpu.VMEM((rows, hidden), BF16),
                pltpu.VMEM((rows, rows), BF16),
                pltpu.VMEM((hidden, rows), BF16),
                pltpu.VMEM((rows, hidden), BF16),
                pltpu.VMEM((rows, 1), F32),
                pltpu.VMEM((rows, hidden), F32),
                pltpu.VMEM((3, nx, hidden, LANE), F32),
                pltpu.VMEM((3, nx, hidden, LANE), BF16),
                pltpu.VMEM((3, nx, hidden, LANE), BF16),
                pltpu.VMEM((nx, half, hidden), F32),
                pltpu.VMEM((nx, half, hidden), BF16),
                pltpu.VMEM((nx, half, hidden), BF16),
                pltpu.VMEM((3, kz, 2, hidden, LANE), BF16),
                pltpu.VMEM((3, kz, 2, hidden, LANE), BF16),
                pltpu.VMEM((kz, 2, half, hidden), BF16),
                pltpu.VMEM((kz, 2, half, hidden), BF16),
                pltpu.VMEM((nx, 8, rows), F32),
                pltpu.VMEM((rows, hidden), BF16),
                pltpu.VMEM((rows, hidden), BF16),
                pltpu.VMEM((STAGES, LANE, hidden), F32),
                dma((6,)),
                dma((6,)),
                dma((2, 2, max(nx, ny))),
                dma((2, 2, max(nx, ny))),
                dma((ny,)),
                dma((ny,)),
                dma((STAGES, steps, 2, 2)),
                dma((STAGES, steps, 2, 2)),
                dma((STAGES, 2)),
                dma((STAGES, 2)),
                dma((STAGES, kz, 2)),
                dma((STAGES, kz, 2)),
                dma((nx,)),
                dma((nx,)),
            ],
            compiler_params=pltpu.CompilerParams(
                collective_id=0, has_side_effects=True, vmem_limit_bytes=60 * 1024 * 1024
            ),
        )(grad_out, expert_ids.T, gate_values.T, pre_gate, pre_up, down_weight)
        return outs[0], outs[1], jnp.swapaxes(outs[2], 1, 2), outs[3]

    placed = (
        P(("dp", "ep"), "tp"),
        P(("dp", "ep"), None),
        P(("dp", "ep"), None),
        P("ep", "dp", "tp"),
        P("ep", "dp", "tp"),
        P("ep", "tp", None),
    )
    return jax.shard_map(
        local,
        mesh=mesh,
        in_specs=placed,
        out_specs=(P("ep", "dp", "tp"), P("ep", "dp", "tp"), P("ep", "tp", "dp"), P("ep", "dp")),
        check_vma=False,
    )
```

```python
import functools

import jax
import jax.numpy as jnp
from jax import lax
from jax.experimental import pallas as pl
from jax.experimental.pallas import tpu as pltpu
from jax.sharding import PartitionSpec as P

MESH = pl.DeviceIdType.MESH
F32 = jnp.float32
BF16 = jnp.bfloat16
LANE = 128
STAGES = 4
ROWS = ((0, 32), (32, 32), (64, 32), (96, 16))
SLAB = 112


def dot(a, b, dims=((1,), (0,))):
    return lax.dot_general(a, b, (dims, ((), ())), preferred_element_type=F32)


def kernel(
    nx, ny, nz,
    grad_hbm, ids_hbm, gate_hbm, pg_hbm, pu_hbm, w_hbm,
    dpg_ref, dpu_ref, down_ref, dgate_ref,
    grad_ref, ids_ref, gate_ref,
    ta, tb, meta, w, pg, pu, act, sm, at, am, gslot, back,
    own, away, mate, own3, away3, mate3,
    out_r, in_r, out_3, in_3, dots,
    sem_local, p1_send, p1_recv, meta_send, meta_recv,
    ag_send, ag_recv, mate_send, mate_recv, rs_send, rs_recv, dot_send, dot_recv,
):
    tok = grad_ref.shape[0]
    rows = ny * tok
    hidden = pg.shape[1]
    x, y, dp = lax.axis_index("tp"), lax.axis_index("ep"), lax.axis_index("dp")
    z, core = dp // 2, dp % 2
    kx, ky, kz = nx // 2, ny // 2, nz // 2
    assert kx == nx // 2 and nx == nz

    def at_x(d):
        return {"tp": lax.rem(x + d + nx, nx)}

    def at_y(d):
        return {"ep": lax.rem(y + d + ny, ny)}

    def at_z(d):
        return {"dp": lax.rem(z + d + nz, nz) * 2 + core}

    other = {"dp": z * 2 + 1 - core}

    barrier = pltpu.get_barrier_semaphore()
    peers = [at_x(k) for k in range(1, nx)] + [at_y(k) for k in range(1, ny)] + [other]
    peers += [at_z(1), at_z(-1)]
    for peer in peers:
        pl.semaphore_signal(barrier, inc=1, device_id=peer, device_id_type=MESH)

    first = [
        pltpu.make_async_copy(grad_hbm, grad_ref, sem_local.at[3]),
        pltpu.make_async_copy(ids_hbm, ids_ref, sem_local.at[4]),
        pltpu.make_async_copy(gate_hbm, gate_ref, sem_local.at[5]),
    ]
    for c in first:
        c.start()
    locals_ = [
        pltpu.make_async_copy(pg_hbm.at[0], pg, sem_local.at[0]),
        pltpu.make_async_copy(pu_hbm.at[0], pu, sem_local.at[1]),
        pltpu.make_async_copy(w_hbm.at[0], w, sem_local.at[2]),
    ]
    for c in locals_:
        c.start()

    for c in first:
        c.wait()
    for s in range(3):
        ta[x, y, 32 * s:32 * s + 32, :] = grad_ref[:, LANE * s:LANE * (s + 1)]
        tb[x, y, 32 * s:32 * s + 32, :] = grad_ref[:, LANE * (s + 4):LANE * (s + 5)]
    ta[x, y, 96:112, :] = grad_ref[0:16, 3 * LANE:4 * LANE]
    tb[x, y, 96:112, :] = grad_ref[16:32, 3 * LANE:4 * LANE]
    labels = lax.broadcasted_iota(jnp.int32, (LANE, tok), 0)
    table = jnp.zeros((LANE, tok), F32)
    gates = gate_ref[...].astype(F32)
    for k in range(ids_ref.shape[0]):
        named = ids_ref[k:k + 1, :]
        table = jnp.where(labels == named, gates[k:k + 1, :], table)
        table = jnp.where(labels == named + 64, 1.0, table)
    meta[y] = table.T.astype(BF16)

    pl.semaphore_wait(barrier, len(peers))

    def p1(path, part, k):
        lo, n = (0, 32) if part == 0 else (32, SLAB - 32)
        buf = ta if path == 0 else tb
        ref = buf.at[x, y, pl.ds(lo, n), :]
        return pltpu.make_async_remote_copy(
            src_ref=ref, dst_ref=ref,
            send_sem=p1_send.at[path, part, k], recv_sem=p1_recv.at[path, part, k],
            device_id=at_y(k) if path == 0 else at_x(k), device_id_type=MESH,
        )

    def meta_copy(k):
        return pltpu.make_async_remote_copy(
            src_ref=meta.at[y], dst_ref=meta.at[y],
            send_sem=meta_send.at[k], recv_sem=meta_recv.at[k],
            device_id=at_y(k), device_id_type=MESH,
        )

    p1_all = [(0, k) for k in range(1, ny)] + [(1, k) for k in range(1, nx)]
    p1_all.sort(key=lambda e: abs(e[1] - (ny if e[0] == 0 else nx) // 2))
    for path, k in p1_all:
        p1(path, 0, k).start()
    for k in range(1, ny):
        meta_copy(k).start()
    for path, k in p1_all:
        p1(path, 1, k).start()

    def ag(s, k, path, right):
        lo, n = ROWS[s]
        last = k == (kx if path == 0 else ky) - 1
        step = -k if right else k
        if path == 0:
            half = ny // 2
            span = pl.ds(0 if right else half, half) if last else pl.ds(0, ny)
            ref = ta.at[lax.rem(x + step + nx, nx), span, pl.ds(lo, n), :]
            to = at_x(1 if right else -1)
        else:
            half = nx // 2
            span = pl.ds(0 if right else half, half) if last else pl.ds(0, nx)
            ref = tb.at[span, lax.rem(y + step + ny, ny), pl.ds(lo, n), :]
            to = at_y(1 if right else -1)
        return pltpu.make_async_remote_copy(
            src_ref=ref, dst_ref=ref,
            send_sem=ag_send.at[s, k, path, int(right)],
            recv_sem=ag_recv.at[s, k, path, int(right)],
            device_id=to, device_id_type=MESH,
        )

    steps = max(kx, ky)

    def streams(k):
        return [(p, r) for p in (0, 1) for r in (True, False) if k < (kx if p == 0 else ky)]

    def ag_start(s, k):
        for p, r in streams(k):
            if k > 0:
                ag(s, k - 1, p, r).wait_recv()
            ag(s, k, p, r).start()

    def ag_finish(s):
        for p in (0, 1):
            for r in (True, False):
                ag(s, (kx if p == 0 else ky) - 1, p, r).wait_recv()

    def prepare():
        locals_[0].wait()
        locals_[1].wait()
        gate_pre = pg[...].astype(F32)
        up_pre = pu[...].astype(F32)
        sigma = jax.nn.sigmoid(gate_pre)
        act[...] = (gate_pre * sigma * up_pre).astype(BF16)
        for k in range(1, ny):
            meta_copy(k).wait_recv()
        tables = meta[...].reshape(rows, LANE)
        tables32 = tables.astype(F32)
        at_row = lax.broadcasted_iota(jnp.int32, (rows, rows), 0)
        at_col = lax.broadcasted_iota(jnp.int32, (rows, rows), 1)
        before = (at_row // tok == at_col // tok) & (at_col < at_row)
        before = jnp.where(before, 1.0, 0.0).astype(BF16)
        ranks = dot(before, tables)
        lane = lax.broadcasted_iota(jnp.int32, (rows, LANE), 1)
        gate_t = jnp.sum(jnp.where(lane == y, tables32, 0.0), axis=1, keepdims=True)
        member = jnp.sum(jnp.where(lane == y + 64, tables32, 0.0), axis=1, keepdims=True)
        rank = jnp.sum(jnp.where(lane == y + 64, ranks, 0.0), axis=1, keepdims=True)
        slot = rank.astype(jnp.int32) + at_row[:, 0:1] // tok * tok
        place = jnp.where(at_col == slot, member, 0.0)
        sm32 = place.T
        sm[...] = sm32.astype(BF16)
        gslot[...] = jnp.sum(
            jnp.where(lane == y, dot(sm[...], tables), 0.0), axis=1, keepdims=True
        )
        moved = dot(place.astype(BF16), act[...]) * gate_t
        am[...] = moved.astype(BF16)
        at[...] = moved.T.astype(BF16)
        back[...] = jnp.zeros_like(back)

    def owner(i):
        return lax.rem(z + lax.select(i % 2 == 1, kz - (i + 1) // 2, i // 2 - kz) + nz, nz)

    def columns(s, i):
        lo, n = ROWS[s]
        a_part, b_part = ta[i, :, lo:lo + n, :], tb[i, :, lo:lo + n, :]
        if s < 3:
            return jnp.concatenate(
                [a_part.reshape(rows, LANE), b_part.reshape(rows, LANE)], axis=1
            )
        return jnp.concatenate([a_part, b_part], axis=1).reshape(rows, LANE)

    def terms(s, lo, hi):
        half = LANE // 2

        def body(i, carry):
            block = columns(s, owner(i))
            if s < 3:
                term = dot(at[...], block)
                first, second = term[:, :LANE], term[:, LANE:]
            else:
                term = dot(block, am[...], ((0,), (0,)))
                first, second = term[:half], term[half:]
            mine = jnp.where(core == 0, first, second)
            theirs = jnp.where(core == 0, second, first).astype(BF16)
            if s < 3:
                own[s, i] = mine
                away[s, i] = theirs
            else:
                own3[i] = mine
                away3[i] = theirs
            return carry
        lax.fori_loop(lo, hi, body, 0, unroll=True)

    def backs(s):
        group = min(4, nx)

        def body(g, carry):
            blocks, weights = [], []
            for j in range(group):
                i = g * group + j
                blocks.append(columns(s, i))
                for tile in (s, s + 4) if s < 3 else (s,):
                    first = pl.multiple_of(i * 7 * LANE + tile * LANE, LANE)
                    weights.append(w[:, pl.ds(first, LANE)])
            back[...] += dot(
                jnp.concatenate(blocks, axis=1), jnp.concatenate(weights, axis=1), ((1,), (1,))
            )
            return carry
        lax.fori_loop(0, nx // group, body, 0)

    cut = min(3, nx - 1)

    def swap(s, part):
        span = pl.ds(0, cut) if part == 0 else pl.ds(cut, nx - cut)
        src, dst = (away.at[s], mate.at[s]) if s < 3 else (away3, mate3)
        return pltpu.make_async_remote_copy(
            src_ref=src.at[span], dst_ref=dst.at[span],
            send_sem=mate_send.at[s, part], recv_sem=mate_recv.at[s, part],
            device_id=other, device_id_type=MESH,
        )

    def rs(s, r, right):
        size = hidden if s < 3 else LANE // 2
        half = size // 2
        if r == 0:
            span = pl.ds(0 if right else half, half)
        else:
            span = pl.ds(0, size)
        d = int(right)
        if s < 3:
            src, dst = out_r.at[s, r, d, span, :], in_r.at[s, r, d, span, :]
        else:
            src, dst = out_3.at[r, d, span, :], in_3.at[r, d, span, :]
        return pltpu.make_async_remote_copy(
            src_ref=src, dst_ref=dst,
            send_sem=rs_send.at[s, r, d], recv_sem=rs_recv.at[s, r, d],
            device_id=at_z(1 if right else -1), device_id_type=MESH,
        )

    def chip_sum(s, i, lo, n):
        if s < 3:
            return own[s, i, lo:lo + n, :] + mate[s, i, lo:lo + n, :].astype(F32)
        return own3[i, lo:lo + n, :] + mate3[i, lo:lo + n, :].astype(F32)

    def came(s, r, d, lo, n):
        if s < 3:
            return in_r[s, r, d, lo:lo + n, :].astype(F32)
        return in_3[r, d, lo:lo + n, :].astype(F32)

    def rs_start(s, r):
        size = hidden if s < 3 else LANE // 2
        half = size // 2
        if r in (0, 2):
            swap(s, r // 2).wait_recv()
        for right in (True, False):
            d = int(right)
            chunk = max(2 * r - d, 0)
            if r > 0:
                rs(s, r - 1, right).wait_recv()
            for lo in (0, half):
                in_half = (lo == 0) == right
                if r == 0 and not in_half:
                    continue
                value = chip_sum(s, chunk, lo, half)
                if r > 1 or (r == 1 and in_half):
                    value = value + came(s, r - 1, d, lo, half)
                if s < 3:
                    out_r[s, r, d, lo:lo + half, :] = value.astype(BF16)
                else:
                    out_3[r, d, lo:lo + half, :] = value.astype(BF16)
            rs(s, r, right).start()

    def rs_finish(s):
        size = hidden if s < 3 else LANE // 2
        half = size // 2
        if kz <= 2:
            swap(s, 1).wait_recv()
        for right in (True, False):
            rs(s, kz - 1, right).wait_recv()
        parts = []
        for lo in (0, half):
            value = chip_sum(s, nz - 1, lo, half)
            for d in (1, 0):
                if kz > 1 or (lo == 0) == (d == 1):
                    value = value + came(s, kz - 1, d, lo, half)
            parts.append(value)
        value = jnp.concatenate(parts, axis=0)
        if s < 3:
            first = pl.multiple_of(LANE * s + core * (LANE // 2), 8)
            down_ref[0, pl.ds(first, LANE), :] = value.T
        else:
            first = pl.multiple_of((1 - core) * 3 * LANE, 8)
            down_ref[0, pl.ds(first, LANE // 2), :] = value

    def dot_copy(k):
        return pltpu.make_async_remote_copy(
            src_ref=dots.at[x], dst_ref=dots.at[x],
            send_sem=dot_send.at[k], recv_sem=dot_recv.at[k],
            device_id=at_x(k), device_id_type=MESH,
        )

    def finish_slots():
        whole = back[...]
        high = whole.astype(BF16)
        low = (whole - high.astype(F32)).astype(BF16)
        placed = dot(sm[...], high) + dot(sm[...], low)
        prod = placed * act[...].astype(F32)
        total = jnp.sum(prod.T, axis=0, keepdims=True)
        dots[x] = jnp.broadcast_to(total, (8, rows))
        for k in range(1, nx):
            dot_copy(k).start()
        gate_pre = pg[...].astype(F32)
        up_pre = pu[...].astype(F32)
        sigma = jax.nn.sigmoid(gate_pre)
        grad_act = gslot[...] * placed
        dpg_ref[0] = (grad_act * up_pre * sigma * (1.0 + gate_pre * (1.0 - sigma))).astype(BF16)
        dpu_ref[0] = (grad_act * (gate_pre * sigma)).astype(BF16)

    def finish_dots():
        for k in range(1, nx):
            dot_copy(k).wait_recv()
        total = dots[0]
        for i in range(1, nx):
            total = total + dots[i]
        dgate_ref[...] = total[0:1, :]

    def multiply(s):
        ag_finish(s)
        if s == 0:
            locals_[2].wait()
        terms(s, 0, cut)
        swap(s, 0).start()
        terms(s, cut, nx)
        swap(s, 1).start()

    def p1_wait(part):
        for path, k in p1_all:
            p1(path, part, k).wait_recv()

    plan = []
    for s in range(STAGES):
        plan += [(k + 0.4 * s, s, ag_start, k) for k in range(steps)]
        plan += [(steps + 0.4 * s, s, multiply, None)]
        plan += [(steps + 0.5 + 0.4 * s + r, s, rs_start, r) for r in range(kz)]
        plan += [(steps + 0.5 + 0.4 * s + kz, s, rs_finish, None)]
    for _, s, step, k in sorted(plan, key=lambda e: e[:2]):
        if step is ag_start and k == 0 and s <= 1:
            p1_wait(s)
        if k is None:
            step(s)
        else:
            step(s, k)
        if step is ag_start and k == 0 and s == 2:
            prepare()
        if step is rs_start and k == min(1, kz - 1):
            backs(s)
            if s == STAGES - 1:
                finish_slots()
    finish_dots()

    for path, k in p1_all:
        for part in (0, 1):
            p1(path, part, k).wait_send()
    for k in range(1, ny):
        meta_copy(k).wait_send()
    for s in range(STAGES):
        for k in range(steps):
            for p, r in streams(k):
                ag(s, k, p, r).wait_send()
        for part in (0, 1):
            swap(s, part).wait_send()
        for r in range(kz):
            for right in (True, False):
                rs(s, r, right).wait_send()
    for k in range(1, nx):
        dot_copy(k).wait_send()


def solution(mesh):
    nx, ny, nz = mesh.shape["tp"], mesh.shape["ep"], mesh.shape["dp"] // 2
    steps = max(nx, ny) // 2

    def local(grad_out, expert_ids, gate_values, pre_gate, pre_up, down_weight):
        rows, hidden = pre_gate.shape[1:]
        width = down_weight.shape[2]
        tok = grad_out.shape[0]
        half = LANE // 2
        kz = nz // 2
        dma = pltpu.SemaphoreType.DMA
        vmem = pl.BlockSpec(memory_space=pltpu.VMEM)
        hbm = pl.BlockSpec(memory_space=pltpu.HBM)
        held = [
            pltpu.with_memory_space_constraint(a, pltpu.HBM)
            for a in (grad_out, expert_ids.T, gate_values.T, pre_gate, pre_up, down_weight)
        ]
        outs = pl.pallas_call(
            functools.partial(kernel, nx, ny, nz),
            out_shape=(
                pltpu.VMEM(pre_gate.shape, BF16),
                pltpu.VMEM(pre_up.shape, BF16),
                pltpu.VMEM((1, width // (2 * nz), hidden), F32),
                pltpu.VMEM((1, rows), F32),
            ),
            in_specs=[hbm] * 6,
            out_specs=(vmem,) * 4,
            scratch_shapes=[
                pltpu.VMEM(grad_out.shape, BF16),
                pltpu.VMEM(expert_ids.shape[::-1], jnp.int32),
                pltpu.VMEM(gate_values.shape[::-1], BF16),
                pltpu.VMEM((nx, ny, SLAB, LANE), BF16),
                pltpu.VMEM((nx, ny, SLAB, LANE), BF16),
                pltpu.VMEM((ny, tok, LANE), BF16),
                pltpu.VMEM((hidden, width), BF16),
                pltpu.VMEM((rows, hidden), BF16),
                pltpu.VMEM((rows, hidden), BF16),
                pltpu.VMEM((rows, hidden), BF16),
                pltpu.VMEM((rows, rows), BF16),
                pltpu.VMEM((hidden, rows), BF16),
                pltpu.VMEM((rows, hidden), BF16),
                pltpu.VMEM((rows, 1), F32),
                pltpu.VMEM((rows, hidden), F32),
                pltpu.VMEM((3, nx, hidden, LANE), F32),
                pltpu.VMEM((3, nx, hidden, LANE), BF16),
                pltpu.VMEM((3, nx, hidden, LANE), BF16),
                pltpu.VMEM((nx, half, hidden), F32),
                pltpu.VMEM((nx, half, hidden), BF16),
                pltpu.VMEM((nx, half, hidden), BF16),
                pltpu.VMEM((3, kz, 2, hidden, LANE), BF16),
                pltpu.VMEM((3, kz, 2, hidden, LANE), BF16),
                pltpu.VMEM((kz, 2, half, hidden), BF16),
                pltpu.VMEM((kz, 2, half, hidden), BF16),
                pltpu.VMEM((nx, 8, rows), F32),
                dma((6,)),
                dma((2, 2, max(nx, ny))),
                dma((2, 2, max(nx, ny))),
                dma((ny,)),
                dma((ny,)),
                dma((STAGES, steps, 2, 2)),
                dma((STAGES, steps, 2, 2)),
                dma((STAGES, 2)),
                dma((STAGES, 2)),
                dma((STAGES, kz, 2)),
                dma((STAGES, kz, 2)),
                dma((nx,)),
                dma((nx,)),
            ],
            compiler_params=pltpu.CompilerParams(
                collective_id=0, has_side_effects=True, vmem_limit_bytes=48 * 1024 * 1024
            ),
        )(*held)
        return outs[0], outs[1], jnp.swapaxes(outs[2], 1, 2), outs[3]

    placed = (
        P(("dp", "ep"), "tp"),
        P(("dp", "ep"), None),
        P(("dp", "ep"), None),
        P("ep", "dp", "tp"),
        P("ep", "dp", "tp"),
        P("ep", "tp", None),
    )
    return jax.shard_map(
        local,
        mesh=mesh,
        in_specs=placed,
        out_specs=(P("ep", "dp", "tp"), P("ep", "dp", "tp"), P("ep", "tp", "dp"), P("ep", "dp")),
        check_vma=False,
    )
```

```python
import functools

import jax
import jax.numpy as jnp
from jax import lax
from jax.experimental import pallas as pl
from jax.experimental.pallas import tpu as pltpu
from jax.sharding import PartitionSpec as P

MESH = pl.DeviceIdType.MESH
F32 = jnp.float32
BF16 = jnp.bfloat16
LANE = 128
STAGES = 4
ROWS = ((0, 32), (32, 32), (64, 32), (96, 16))
SLAB = 112
PARTS = ((0, 64), (64, 48))


def dot(a, b, dims=((1,), (0,))):
    return lax.dot_general(a, b, (dims, ((), ())), preferred_element_type=F32)


def kernel(
    nx, ny, nz,
    grad_hbm, ids_hbm, gate_hbm, pg_hbm, pu_hbm, w_hbm,
    dpg_ref, dpu_ref, down_ref, dgate_ref,
    grad_ref, ids_ref, gate_ref,
    ta, tb, meta, w, pg, pu, act, sm, at, am, gslot, back,
    own, away, mate, own3, away3, mate3,
    out_r, in_r, out_3, in_3, dots,
    sem_local, p1_send, p1_recv, meta_send, meta_recv,
    ag_send, ag_recv, mate_send, mate_recv, rs_send, rs_recv, dot_send, dot_recv,
):
    tok = grad_ref.shape[0]
    rows = ny * tok
    hidden = pg.shape[1]
    x, y, dp = lax.axis_index("tp"), lax.axis_index("ep"), lax.axis_index("dp")
    z, core = dp // 2, dp % 2
    kx, ky, kz = nx // 2, ny // 2, nz // 2
    assert kx == nx // 2 and nx == nz

    def at_x(d):
        return {"tp": lax.rem(x + d + nx, nx)}

    def at_y(d):
        return {"ep": lax.rem(y + d + ny, ny)}

    def at_z(d):
        return {"dp": lax.rem(z + d + nz, nz) * 2 + core}

    other = {"dp": z * 2 + 1 - core}

    barrier = pltpu.get_barrier_semaphore()
    peers = [at_x(k) for k in range(1, nx)] + [at_y(k) for k in range(1, ny)] + [other]
    peers += [at_z(1), at_z(-1)]
    for peer in peers:
        pl.semaphore_signal(barrier, inc=1, device_id=peer, device_id_type=MESH)

    first = [
        pltpu.make_async_copy(grad_hbm, grad_ref, sem_local.at[3]),
        pltpu.make_async_copy(ids_hbm, ids_ref, sem_local.at[4]),
        pltpu.make_async_copy(gate_hbm, gate_ref, sem_local.at[5]),
    ]
    for c in first:
        c.start()
    locals_ = [
        pltpu.make_async_copy(pg_hbm.at[0], pg, sem_local.at[0]),
        pltpu.make_async_copy(pu_hbm.at[0], pu, sem_local.at[1]),
        pltpu.make_async_copy(w_hbm.at[0], w, sem_local.at[2]),
    ]
    for c in locals_:
        c.start()

    for c in first:
        c.wait()
    for s in range(3):
        ta[x, y, 32 * s:32 * s + 32, :] = grad_ref[:, LANE * s:LANE * (s + 1)]
        tb[x, y, 32 * s:32 * s + 32, :] = grad_ref[:, LANE * (s + 4):LANE * (s + 5)]
    ta[x, y, 96:112, :] = grad_ref[0:16, 3 * LANE:4 * LANE]
    tb[x, y, 96:112, :] = grad_ref[16:32, 3 * LANE:4 * LANE]
    labels = lax.broadcasted_iota(jnp.int32, (LANE, tok), 0)
    table = jnp.zeros((LANE, tok), F32)
    gates = gate_ref[...].astype(F32)
    for k in range(ids_ref.shape[0]):
        named = ids_ref[k:k + 1, :]
        table = jnp.where(labels == named, gates[k:k + 1, :], table)
        table = jnp.where(labels == named + 64, 1.0, table)
    meta[y] = table.T.astype(BF16)

    pl.semaphore_wait(barrier, len(peers))

    def p1(path, part, k):
        lo, n = PARTS[part]
        buf = ta if path == 0 else tb
        ref = buf.at[x, y, pl.ds(lo, n), :]
        return pltpu.make_async_remote_copy(
            src_ref=ref, dst_ref=ref,
            send_sem=p1_send.at[path, part, k], recv_sem=p1_recv.at[path, part, k],
            device_id=at_y(k) if path == 0 else at_x(k), device_id_type=MESH,
        )

    def meta_copy(k):
        return pltpu.make_async_remote_copy(
            src_ref=meta.at[y], dst_ref=meta.at[y],
            send_sem=meta_send.at[k], recv_sem=meta_recv.at[k],
            device_id=at_y(k), device_id_type=MESH,
        )

    p1_all = [(0, k) for k in range(1, ny)] + [(1, k) for k in range(1, nx)]
    p1_all.sort(key=lambda e: abs(e[1] - (ny if e[0] == 0 else nx) // 2))
    for path, k in p1_all:
        p1(path, 0, k).start()
    for k in range(1, ny):
        meta_copy(k).start()
    for part in range(1, len(PARTS)):
        for path, k in p1_all:
            p1(path, part, k).start()

    def ag(s, k, path, right):
        lo, n = ROWS[s]
        last = k == (kx if path == 0 else ky) - 1
        step = -k if right else k
        if path == 0:
            half = ny // 2
            span = pl.ds(0 if right else half, half) if last else pl.ds(0, ny)
            ref = ta.at[lax.rem(x + step + nx, nx), span, pl.ds(lo, n), :]
            to = at_x(1 if right else -1)
        else:
            half = nx // 2
            span = pl.ds(0 if right else half, half) if last else pl.ds(0, nx)
            ref = tb.at[span, lax.rem(y + step + ny, ny), pl.ds(lo, n), :]
            to = at_y(1 if right else -1)
        return pltpu.make_async_remote_copy(
            src_ref=ref, dst_ref=ref,
            send_sem=ag_send.at[s, k, path, int(right)],
            recv_sem=ag_recv.at[s, k, path, int(right)],
            device_id=to, device_id_type=MESH,
        )

    steps = max(kx, ky)

    def streams(k):
        return [(p, r) for p in (0, 1) for r in (True, False) if k < (kx if p == 0 else ky)]

    def ag_start(s, k):
        for p, r in streams(k):
            if k > 0:
                ag(s, k - 1, p, r).wait_recv()
            ag(s, k, p, r).start()

    def ag_finish(s):
        for p in (0, 1):
            for r in (True, False):
                ag(s, (kx if p == 0 else ky) - 1, p, r).wait_recv()

    def prepare():
        locals_[0].wait()
        locals_[1].wait()
        gate_pre = pg[...].astype(F32)
        up_pre = pu[...].astype(F32)
        sigma = jax.nn.sigmoid(gate_pre)
        act[...] = (gate_pre * sigma * up_pre).astype(BF16)
        for k in range(1, ny):
            meta_copy(k).wait_recv()
        tables = meta[...].reshape(rows, LANE)
        tables32 = tables.astype(F32)
        at_row = lax.broadcasted_iota(jnp.int32, (rows, rows), 0)
        at_col = lax.broadcasted_iota(jnp.int32, (rows, rows), 1)
        before = (at_row // tok == at_col // tok) & (at_col < at_row)
        before = jnp.where(before, 1.0, 0.0).astype(BF16)
        ranks = dot(before, tables)
        lane = lax.broadcasted_iota(jnp.int32, (rows, LANE), 1)
        gate_t = jnp.sum(jnp.where(lane == y, tables32, 0.0), axis=1, keepdims=True)
        member = jnp.sum(jnp.where(lane == y + 64, tables32, 0.0), axis=1, keepdims=True)
        rank = jnp.sum(jnp.where(lane == y + 64, ranks, 0.0), axis=1, keepdims=True)
        slot = rank.astype(jnp.int32) + at_row[:, 0:1] // tok * tok
        place = jnp.where(at_col == slot, member, 0.0)
        sm32 = place.T
        sm[...] = sm32.astype(BF16)
        gslot[...] = jnp.sum(
            jnp.where(lane == y, dot(sm[...], tables), 0.0), axis=1, keepdims=True
        )
        moved = dot(place.astype(BF16), act[...]) * gate_t
        am[...] = moved.astype(BF16)
        at[...] = moved.T.astype(BF16)
        back[...] = jnp.zeros_like(back)

    def owner(i):
        return lax.rem(z + lax.select(i % 2 == 1, kz - (i + 1) // 2, i // 2 - kz) + nz, nz)

    def columns(s, i):
        lo, n = ROWS[s]
        a_part, b_part = ta[i, :, lo:lo + n, :], tb[i, :, lo:lo + n, :]
        if s < 3:
            return jnp.concatenate(
                [a_part.reshape(rows, LANE), b_part.reshape(rows, LANE)], axis=1
            )
        return jnp.concatenate([a_part, b_part], axis=1).reshape(rows, LANE)

    def terms(s, lo, hi):
        half = LANE // 2

        def body(i, carry):
            block = columns(s, owner(i))
            if s < 3:
                term = dot(at[...], block)
                first, second = term[:, :LANE], term[:, LANE:]
            else:
                term = dot(block, am[...], ((0,), (0,)))
                first, second = term[:half], term[half:]
            mine = jnp.where(core == 0, first, second)
            theirs = jnp.where(core == 0, second, first).astype(BF16)
            if s < 3:
                own[s, i] = mine
                away[s, i] = theirs
            else:
                own3[i] = mine
                away3[i] = theirs
            return carry
        lax.fori_loop(lo, hi, body, 0, unroll=True)

    def backs(s):
        group = min(4, nx)

        def body(g, carry):
            blocks, weights = [], []
            for j in range(group):
                i = g * group + j
                blocks.append(columns(s, i))
                for tile in (s, s + 4) if s < 3 else (s,):
                    first = pl.multiple_of(i * 7 * LANE + tile * LANE, LANE)
                    weights.append(w[:, pl.ds(first, LANE)])
            back[...] += dot(
                jnp.concatenate(blocks, axis=1), jnp.concatenate(weights, axis=1), ((1,), (1,))
            )
            return carry
        lax.fori_loop(0, nx // group, body, 0)

    cut = min(3, nx - 1)

    def swap(s, part):
        span = pl.ds(0, cut) if part == 0 else pl.ds(cut, nx - cut)
        src, dst = (away.at[s], mate.at[s]) if s < 3 else (away3, mate3)
        return pltpu.make_async_remote_copy(
            src_ref=src.at[span], dst_ref=dst.at[span],
            send_sem=mate_send.at[s, part], recv_sem=mate_recv.at[s, part],
            device_id=other, device_id_type=MESH,
        )

    def rs(s, r, right):
        size = hidden if s < 3 else LANE // 2
        half = size // 2
        if r == 0:
            span = pl.ds(0 if right else half, half)
        else:
            span = pl.ds(0, size)
        d = int(right)
        if s < 3:
            src, dst = out_r.at[s, r, d, span, :], in_r.at[s, r, d, span, :]
        else:
            src, dst = out_3.at[r, d, span, :], in_3.at[r, d, span, :]
        return pltpu.make_async_remote_copy(
            src_ref=src, dst_ref=dst,
            send_sem=rs_send.at[s, r, d], recv_sem=rs_recv.at[s, r, d],
            device_id=at_z(1 if right else -1), device_id_type=MESH,
        )

    def chip_sum(s, i, lo, n):
        if s < 3:
            return own[s, i, lo:lo + n, :] + mate[s, i, lo:lo + n, :].astype(F32)
        return own3[i, lo:lo + n, :] + mate3[i, lo:lo + n, :].astype(F32)

    def came(s, r, d, lo, n):
        if s < 3:
            return in_r[s, r, d, lo:lo + n, :].astype(F32)
        return in_3[r, d, lo:lo + n, :].astype(F32)

    def rs_start(s, r):
        size = hidden if s < 3 else LANE // 2
        half = size // 2
        if r in (0, 2):
            swap(s, r // 2).wait_recv()
        for right in (True, False):
            d = int(right)
            chunk = max(2 * r - d, 0)
            if r > 0:
                rs(s, r - 1, right).wait_recv()
            for lo in (0, half):
                in_half = (lo == 0) == right
                if r == 0 and not in_half:
                    continue
                value = chip_sum(s, chunk, lo, half)
                if r > 1 or (r == 1 and in_half):
                    value = value + came(s, r - 1, d, lo, half)
                if s < 3:
                    out_r[s, r, d, lo:lo + half, :] = value.astype(BF16)
                else:
                    out_3[r, d, lo:lo + half, :] = value.astype(BF16)
            rs(s, r, right).start()

    def rs_finish(s):
        size = hidden if s < 3 else LANE // 2
        half = size // 2
        if kz <= 2:
            swap(s, 1).wait_recv()
        for right in (True, False):
            rs(s, kz - 1, right).wait_recv()
        parts = []
        for lo in (0, half):
            value = chip_sum(s, nz - 1, lo, half)
            for d in (1, 0):
                if kz > 1 or (lo == 0) == (d == 1):
                    value = value + came(s, kz - 1, d, lo, half)
            parts.append(value)
        value = jnp.concatenate(parts, axis=0)
        if s < 3:
            first = pl.multiple_of(LANE * s + core * (LANE // 2), 8)
            down_ref[0, pl.ds(first, LANE), :] = value.T
        else:
            first = pl.multiple_of((1 - core) * 3 * LANE, 8)
            down_ref[0, pl.ds(first, LANE // 2), :] = value

    def dot_copy(k):
        return pltpu.make_async_remote_copy(
            src_ref=dots.at[x], dst_ref=dots.at[x],
            send_sem=dot_send.at[k], recv_sem=dot_recv.at[k],
            device_id=at_x(k), device_id_type=MESH,
        )

    def finish_slots():
        whole = back[...]
        high = whole.astype(BF16)
        low = (whole - high.astype(F32)).astype(BF16)
        placed = dot(sm[...], high) + dot(sm[...], low)
        prod = placed * act[...].astype(F32)
        total = jnp.sum(prod.T, axis=0, keepdims=True)
        dots[x] = jnp.broadcast_to(total, (8, rows))
        for k in range(1, nx):
            dot_copy(k).start()
        gate_pre = pg[...].astype(F32)
        up_pre = pu[...].astype(F32)
        sigma = jax.nn.sigmoid(gate_pre)
        grad_act = gslot[...] * placed
        dpg_ref[0] = (grad_act * up_pre * sigma * (1.0 + gate_pre * (1.0 - sigma))).astype(BF16)
        dpu_ref[0] = (grad_act * (gate_pre * sigma)).astype(BF16)

    def finish_dots():
        for k in range(1, nx):
            dot_copy(k).wait_recv()
        total = dots[0]
        for i in range(1, nx):
            total = total + dots[i]
        dgate_ref[...] = total[0:1, :]

    def multiply(s):
        ag_finish(s)
        if s == 0:
            locals_[2].wait()
        terms(s, 0, cut)
        swap(s, 0).start()
        terms(s, cut, nx)
        swap(s, 1).start()

    def p1_wait(part):
        for path, k in p1_all:
            p1(path, part, k).wait_recv()

    def drain():
        for path, k in p1_all:
            for part in range(len(PARTS)):
                p1(path, part, k).wait_send()
        for k in range(1, ny):
            meta_copy(k).wait_send()
        for s in range(STAGES):
            for k in range(steps):
                for p, r in streams(k):
                    ag(s, k, p, r).wait_send()
            for part in (0, 1):
                swap(s, part).wait_send()
            for r in range(kz - 1):
                for right in (True, False):
                    rs(s, r, right).wait_send()

    plan = []
    for s in range(STAGES):
        plan += [(k + 0.4 * s, s, ag_start, k) for k in range(steps)]
        plan += [(steps + 0.4 * s, s, multiply, None)]
        plan += [(steps + 0.5 + 0.4 * s + r, s, rs_start, r) for r in range(kz)]
        plan += [(steps + 0.5 + 0.4 * s + kz, s, rs_finish, None)]
    for _, s, step, k in sorted(plan, key=lambda e: e[:2]):
        if step is ag_start and k == 0:
            for part, (lo, _) in enumerate(PARTS):
                if lo == ROWS[s][0]:
                    p1_wait(part)
        if k is None:
            step(s)
        else:
            step(s, k)
        if step is ag_start and k == 0 and s == 2:
            prepare()
        if step is rs_start and k == min(1, kz - 1):
            backs(s)
            if s == STAGES - 1:
                finish_slots()
        if step is rs_start and k == kz - 1 and s == STAGES - 1:
            drain()
    finish_dots()

    for s in range(STAGES):
        for right in (True, False):
            rs(s, kz - 1, right).wait_send()
    for k in range(1, nx):
        dot_copy(k).wait_send()


def solution(mesh):
    nx, ny, nz = mesh.shape["tp"], mesh.shape["ep"], mesh.shape["dp"] // 2
    steps = max(nx, ny) // 2

    def local(grad_out, expert_ids, gate_values, pre_gate, pre_up, down_weight):
        rows, hidden = pre_gate.shape[1:]
        width = down_weight.shape[2]
        tok = grad_out.shape[0]
        half = LANE // 2
        kz = nz // 2
        dma = pltpu.SemaphoreType.DMA
        vmem = pl.BlockSpec(memory_space=pltpu.VMEM)
        hbm = pl.BlockSpec(memory_space=pltpu.HBM)
        held = [
            pltpu.with_memory_space_constraint(a, pltpu.HBM)
            for a in (grad_out, expert_ids.T, gate_values.T, pre_gate, pre_up, down_weight)
        ]
        outs = pl.pallas_call(
            functools.partial(kernel, nx, ny, nz),
            out_shape=(
                pltpu.VMEM(pre_gate.shape, BF16),
                pltpu.VMEM(pre_up.shape, BF16),
                pltpu.VMEM((1, width // (2 * nz), hidden), F32),
                pltpu.VMEM((1, rows), F32),
            ),
            in_specs=[hbm] * 6,
            out_specs=(vmem,) * 4,
            scratch_shapes=[
                pltpu.VMEM(grad_out.shape, BF16),
                pltpu.VMEM(expert_ids.shape[::-1], jnp.int32),
                pltpu.VMEM(gate_values.shape[::-1], BF16),
                pltpu.VMEM((nx, ny, SLAB, LANE), BF16),
                pltpu.VMEM((nx, ny, SLAB, LANE), BF16),
                pltpu.VMEM((ny, tok, LANE), BF16),
                pltpu.VMEM((hidden, width), BF16),
                pltpu.VMEM((rows, hidden), BF16),
                pltpu.VMEM((rows, hidden), BF16),
                pltpu.VMEM((rows, hidden), BF16),
                pltpu.VMEM((rows, rows), BF16),
                pltpu.VMEM((hidden, rows), BF16),
                pltpu.VMEM((rows, hidden), BF16),
                pltpu.VMEM((rows, 1), F32),
                pltpu.VMEM((rows, hidden), F32),
                pltpu.VMEM((3, nx, hidden, LANE), F32),
                pltpu.VMEM((3, nx, hidden, LANE), BF16),
                pltpu.VMEM((3, nx, hidden, LANE), BF16),
                pltpu.VMEM((nx, half, hidden), F32),
                pltpu.VMEM((nx, half, hidden), BF16),
                pltpu.VMEM((nx, half, hidden), BF16),
                pltpu.VMEM((3, kz, 2, hidden, LANE), BF16),
                pltpu.VMEM((3, kz, 2, hidden, LANE), BF16),
                pltpu.VMEM((kz, 2, half, hidden), BF16),
                pltpu.VMEM((kz, 2, half, hidden), BF16),
                pltpu.VMEM((nx, 8, rows), F32),
                dma((6,)),
                dma((2, len(PARTS), max(nx, ny))),
                dma((2, len(PARTS), max(nx, ny))),
                dma((ny,)),
                dma((ny,)),
                dma((STAGES, steps, 2, 2)),
                dma((STAGES, steps, 2, 2)),
                dma((STAGES, 2)),
                dma((STAGES, 2)),
                dma((STAGES, kz, 2)),
                dma((STAGES, kz, 2)),
                dma((nx,)),
                dma((nx,)),
            ],
            compiler_params=pltpu.CompilerParams(
                collective_id=0, has_side_effects=True, vmem_limit_bytes=48 * 1024 * 1024
            ),
        )(*held)
        return outs[0], outs[1], jnp.swapaxes(outs[2], 1, 2), outs[3]

    placed = (
        P(("dp", "ep"), "tp"),
        P(("dp", "ep"), None),
        P(("dp", "ep"), None),
        P("ep", "dp", "tp"),
        P("ep", "dp", "tp"),
        P("ep", "tp", None),
    )
    return jax.shard_map(
        local,
        mesh=mesh,
        in_specs=placed,
        out_specs=(P("ep", "dp", "tp"), P("ep", "dp", "tp"), P("ep", "tp", "dp"), P("ep", "dp")),
        check_vma=False,
    )
```
